32 devices in a mesh: groups: 2 (over y), pre: 4 (over z), post: 2 (over x), rep: 2 (over core).
Axes of the slice: x: 2, y: 2, z: 4, core: 2. Of those that a mesh axis runs over, the one named last changes fastest.
Arguments:
- rates0: bfloat16 [256, 2048], P(('groups', 'rep'), 'pre'), parts along dimension 0, may hold values from -0.94921875 to 0.94921875
- stimulus: bfloat16 [256, 2048], P(('groups', 'rep'), 'post'), parts along dimension 0, may hold values from -6 to 6
- cotangent: bfloat16 [256, 2048], P(('groups', 'rep'), 'post'), parts along dimension 0, may hold values from -6 to 6
- weights: bfloat16 [8, 2, 64, 128, 128], P(('groups', 'pre'), 'post'), parts along dimension 0, may hold values from -0.375 to 0.375
- src_block: int32 [8, 2, 64], P(('groups', 'pre'), 'post'), parts along dimension 0, may hold values from 0 to 3
- dst_block: int32 [8, 2, 64], P(('groups', 'pre'), 'post'), parts along dimension 0, may hold values from 0 to 7
- live_count: int32 [8, 2], P(('groups', 'pre'), 'post'), parts along dimension 0, may hold values from 16 to 64, as said below
- cell_type: int32 [4096], P(('groups', 'post')), parts along dimension 0, may hold values from 0 to 31
- gains: float32 [32], replicated, may hold values from 0.5 to 2
Outputs:
- final_rates: bfloat16 [256, 2048], P(('groups', 'rep'), 'post'), parts along dimension 0
- grad_weight: float32 [8, 2, 64, 128, 128], P(('groups', 'pre'), 'post', 'rep'), parts along dimension 0
- grad_gain: float32 [64], P('groups'), parts along dimension 0
The draws below stay inside these ranges and needn't reach their ends.
There are 2 independent parts, one for each index of `groups`. The reference program is written for one: setup_inputs(seed, part) draws one part's arguments, and reference() takes and returns one part's arrays. A program takes and returns all parts, laid end to end along the dimension named above; an argument that names none is the same for every part. Nothing has to cross between parts.
Inputs may be any that keep to these rules, and one draw needn't show every extreme that they name: Slots from live_count on are unused; some tile of every draw uses all 64 slots.
All inputs are finite; a program needn't handle non-finite values.
Results may differ from the reference program's by a relative error of at most 0.035.
Values may be sent and summed in bfloat16 or wider, within the bound.
A program may use at most 64 MiB of HBM per device.

```python
import math
import jax
import jax.numpy as jnp
import numpy as np
from jax import lax

BS = 128
NEUR = 2048
NTYPES = 32
STEPS = 4
KB = 64
BATCH = 128
NB_PRE = 4
NB_POST = 8
N_PRE = 4
N_POST = 2


def draw_live_count(key, part):
    key = jax.random.fold_in(key, 7)
    first, second = jax.random.split(key)
    counts = jax.random.randint(first, (N_PRE * N_POST,), KB // 4, KB + 1)
    chosen = jax.random.randint(second, (), 0, N_PRE * N_POST)
    filled = jnp.where(jnp.arange(N_PRE * N_POST) == chosen, KB, counts)
    return filled.reshape(N_PRE, N_POST).astype(jnp.int32)


def set_ends(values, key, smallest, top_value):
    spot = [jax.random.randint(jax.random.fold_in(key, axis), (), 0, length) for axis, length in enumerate(values.shape)]
    longest = values.shape.index(max(values.shape))
    neighbour = spot[:longest] + [(spot[longest] + 1) % values.shape[longest]] + spot[longest + 1:]
    return values.at[tuple(spot)].set(smallest).at[tuple(neighbour)].set(top_value)


def steps_of(stream_key, extent, cuts, least, largest):
    factor_of = 1.0
    for position, blocks in cuts:
        steps = jax.random.uniform(jax.random.fold_in(jax.random.fold_in(stream_key, 6), position), (blocks,), jnp.float32, least / len(cuts), largest / len(cuts))
        factor_of = factor_of * jnp.repeat(jnp.exp(steps), extent[position] // blocks).reshape((-1,) + (1,) * (len(extent) - 1 - position))
    return factor_of


def rank_table(number_of, lean):
    loads = [(1 << 20) // math.isqrt(standing ** lean) + 1 for standing in range(1, number_of + 1)]
    deviation = 1 + sum(loads) // (1 << 30)
    return np.cumsum(np.array([max(1, weight // deviation) for weight in loads]))


def ranked_ids(own_key, extent, number_of, slope):
    listing = rank_table(number_of, slope)
    lot = jax.random.randint(jax.random.fold_in(own_key, 1), extent, 0, int(listing[number_of - 1]))
    standing = jnp.searchsorted(jnp.asarray(listing, jnp.int32), lot, side="right")
    return jax.random.permutation(jax.random.fold_in(own_key, 2), number_of)[standing].astype(jnp.int32)


def centred(key, dims, width, most, cuts=(), kind=jnp.bfloat16):
    entries = jax.random.normal(key, dims, jnp.float32) * width
    if len(cuts) > 0:
        entries = steps_of(key, dims, cuts, -0.22, 0.18) * entries
    return jnp.clip(entries, min=-most, max=most).astype(kind)


def setup_inputs(seed: int = 0, part: int = 0) -> dict:
    keys = jax.random.split(jax.random.key(seed), 10)
    own_keys = jax.random.split(jax.random.fold_in(keys[9], part), 10)
    rates0 = jnp.clip(jax.random.uniform(own_keys[0], (BATCH, NEUR), jnp.float32, -0.94921875, 0.94921875) * steps_of(own_keys[0], (BATCH, NEUR), ((0, 2), (1, 4)), -0.4, 0.0), -0.94921875, 0.94921875).astype(jnp.bfloat16)
    stimulus = centred(own_keys[1], (BATCH, NEUR), 1.0, 6.0, ((0, 2), (1, 2)))
    cotangent = centred(own_keys[2], (BATCH, NEUR), 1.0, 6.0, ((0, 2), (1, 2)))
    weights = centred(own_keys[3], (N_PRE, N_POST, KB, BS, BS), (2 * BS) ** -0.5, 0.375, ((0, 4), (1, 2)))
    src_block = set_ends(jax.random.randint(own_keys[4], (N_PRE, N_POST, KB), 0, NB_PRE), jax.random.fold_in(own_keys[4], 1), 0, NB_PRE - 1).astype(jnp.int32)
    dst_block = set_ends(ranked_ids(own_keys[5], (N_PRE, N_POST, KB), NB_POST, 2), jax.random.fold_in(own_keys[5], 3), 0, NB_POST - 1).astype(jnp.int32)
    live_count = draw_live_count(jax.random.fold_in(jax.random.fold_in(keys[9], part), 71), part)
    cell_type = set_ends(jax.random.randint(own_keys[7], (NEUR,), 0, NTYPES), jax.random.fold_in(own_keys[7], 1), 0, NTYPES - 1).astype(jnp.int32)
    gains = jnp.clip(jnp.exp(jax.random.uniform(keys[8], (NTYPES,), jnp.float32, math.log(0.5), math.log(2.0))), 0.5, 2.0)
    return {"rates0": rates0, "stimulus": stimulus, "cotangent": cotangent, "weights": weights, "src_block": src_block, "dst_block": dst_block, "live_count": live_count, "cell_type": cell_type, "gains": gains}


leak_rate = 0.35

def tile_forward(rates_slice, blocks, sources, targets):
    rows = rates_slice.shape[0]
    grid = rates_slice.reshape(rows, -1, BS)
    picked = jnp.take(grid, sources, axis=1)
    prod = jnp.einsum('bkp,kpq->kbq', picked.astype(jnp.float32), blocks.astype(jnp.float32))
    summed = jax.ops.segment_sum(prod, targets, num_segments=NB_POST)
    return jnp.transpose(summed, (1, 0, 2)).reshape(rows, NB_POST * BS)

def tile_backward(delta_slice, blocks, sources, targets):
    rows = delta_slice.shape[0]
    grid = delta_slice.reshape(rows, -1, BS)
    picked = jnp.take(grid, targets, axis=1)
    prod = jnp.einsum('bkq,kpq->kbp', picked.astype(jnp.float32), blocks.astype(jnp.float32))
    summed = jax.ops.segment_sum(prod, sources, num_segments=NB_PRE)
    return jnp.transpose(summed, (1, 0, 2)).reshape(rows, NB_PRE * BS)

def tile_grad(rates_slice, delta_slice, sources, targets):
    rows = rates_slice.shape[0]
    picked_rates = jnp.take(rates_slice.reshape(rows, -1, BS), sources, axis=1)
    picked_delta = jnp.take(delta_slice.reshape(rows, -1, BS), targets, axis=1)
    return jnp.einsum('bkp,bkq->kpq', picked_rates.astype(jnp.float32), picked_delta.astype(jnp.float32))

def reference(rates0, stimulus, cotangent, weights, src_block, dst_block, live_count, cell_type, gains):
    n_pre = NEUR // N_PRE
    n_post = NEUR // N_POST
    rows = rates0.shape[0]
    slot_mask = jnp.arange(KB, dtype=jnp.int32)[None, None, :] < live_count[:, :, None]
    used = weights * slot_mask.astype(jnp.bfloat16)[:, :, :, None, None]
    neuron_gain = gains[cell_type]

    def currents(rates):

        def add_tile(total, inputs):
            piece, blocks, sources, targets = inputs
            rates_slice = lax.dynamic_slice_in_dim(rates, piece * n_pre, n_pre, 1)
            parts = jax.vmap(lambda b, s, d: tile_forward(rates_slice, b, s, d))(blocks, sources, targets)
            parts = jnp.transpose(parts, (1, 0, 2)).reshape(rows, NEUR)
            rounded = lax.optimization_barrier(parts.astype(jnp.bfloat16))
            return (total + rounded.astype(jnp.float32), None)
        pieces = jnp.arange(N_PRE, dtype=jnp.int32)
        total, _ = lax.scan(add_tile, jnp.zeros((rows, NEUR), jnp.float32), (pieces, used, src_block, dst_block))
        return total

    def backs(delta):

        def add_tile(total, inputs):
            piece, blocks, sources, targets = inputs
            delta_slice = lax.dynamic_slice_in_dim(delta, piece * n_post, n_post, 1)
            parts = jax.vmap(lambda b, s, d: tile_backward(delta_slice, b, s, d))(blocks, sources, targets)
            parts = jnp.transpose(parts, (1, 0, 2)).reshape(rows, NEUR)
            rounded = lax.optimization_barrier(parts.astype(jnp.bfloat16))
            return (total + rounded.astype(jnp.float32), None)
        pieces = jnp.arange(N_POST, dtype=jnp.int32)
        total, _ = lax.scan(add_tile, jnp.zeros((rows, NEUR), jnp.float32), (pieces, jnp.swapaxes(used, 0, 1), jnp.swapaxes(src_block, 0, 1), jnp.swapaxes(dst_block, 0, 1)))
        return total

    def grads(rates, delta):
        rate_tiles = jnp.transpose(rates.reshape(rows, N_PRE, n_pre), (1, 0, 2))
        delta_tiles = jnp.transpose(delta.reshape(rows, N_POST, n_post), (1, 0, 2))

        def one_row(carry, inputs):
            rate_tile, source_row, target_row = inputs
            out = jax.vmap(lambda dl, s, d: tile_grad(rate_tile, dl, s, d))(delta_tiles, source_row, target_row)
            return (carry, out)
        _, result = lax.scan(one_row, jnp.zeros((), jnp.float32), (rate_tiles, src_block, dst_block))
        return result
    rates = rates0
    saved_rates = []
    saved_act = []
    saved_cur = []
    for step in range(STEPS):
        cur = currents(rates)
        act = jnp.tanh(neuron_gain * cur + stimulus.astype(jnp.float32))
        saved_rates.append(rates)
        saved_act.append(act)
        saved_cur.append(cur)
        rates = ((1.0 - leak_rate) * rates.astype(jnp.float32) + leak_rate * act).astype(jnp.bfloat16)
    final_rates = rates
    error = cotangent.astype(jnp.float32)
    grad_weight = jnp.zeros(weights.shape, jnp.float32)
    grad_gain = jnp.zeros((NTYPES,), jnp.float32)
    for step in reversed(range(STEPS)):
        act = saved_act[step]
        du = error * leak_rate * (1.0 - act * act)
        grad_gain = grad_gain + jax.ops.segment_sum(lax.optimization_barrier(jnp.sum(du * saved_cur[step], axis=0)), cell_type, num_segments=NTYPES)
        dcur = (du * neuron_gain).astype(jnp.bfloat16)
        grad_weight = grad_weight + grads(saved_rates[step], dcur)
        if step > 0:
            error = (1.0 - leak_rate) * error + backs(dcur)
    grad_weight = grad_weight * slot_mask.astype(jnp.float32)[:, :, :, None, None]
    return (final_rates, grad_weight, grad_gain)
```

```python
import functools

import jax
import jax.numpy as jnp
from jax import lax
from jax.experimental import pallas as pl
from jax.experimental.pallas import tpu as pltpu
from jax.sharding import PartitionSpec as P

STEPS = 4
LEAK = 0.35
MESH = pl.DeviceIdType.MESH
F32 = jnp.float32
BF16 = jnp.bfloat16
CHUNK = 8


def build_kernel(src_ref, dst_ref, live_ref, w_ref, out_ref, acc):
    width = w_ref.shape[-1]
    part = pl.program_id(0)

    @pl.when(part == 0)
    def _():
        acc[...] = jnp.zeros_like(acc)

    live = live_ref[0, 0]
    for s in range(CHUNK):
        k = part * CHUNK + s

        @pl.when(k < live)
        def _():
            rows = pl.ds(pl.multiple_of(src_ref[0, 0, k] * width, width), width)
            cols = pl.ds(pl.multiple_of(dst_ref[0, 0, k] * width, width), width)
            acc[rows, cols] += w_ref[0, 0, s].astype(F32)

    @pl.when(part == pl.num_programs(0) - 1)
    def _():
        out_ref[...] = acc[...].astype(BF16)


def emit_kernel(src_ref, dst_ref, live_ref, g_ref, out_ref, zero, sem):
    width = zero.shape[0]
    share = out_ref.shape[2]
    first = lax.axis_index("rep") * share
    live = live_ref[0, 0]
    zero[...] = jnp.zeros_like(zero)

    def start(k, carry):
        slot = first + k

        @pl.when(slot < live)
        def _():
            rows = pl.ds(pl.multiple_of(src_ref[0, 0, slot] * width, width), width)
            cols = pl.ds(pl.multiple_of(dst_ref[0, 0, slot] * width, width), width)
            pltpu.make_async_copy(g_ref.at[rows, cols], out_ref.at[0, 0, k], sem.at[k]).start()

        @pl.when(slot >= live)
        def _():
            pltpu.make_async_copy(zero, out_ref.at[0, 0, k], sem.at[k]).start()

        return carry

    lax.fori_loop(0, share, start, 0)

    def finish(k, carry):
        pltpu.make_async_copy(zero, out_ref.at[0, 0, k], sem.at[k]).wait()
        return carry

    lax.fori_loop(0, share, finish, 0)


def step_kernel(
    sizes,
    rates_ref, stim_ref, cot_ref, w_ref, ct_ref, gains_ref,
    final_ref, gg_ref, g_ref,
    rbuf, dbuf, fbuf, psend, precv, dsend, bsend, brecv, stage, sbuf, ctsend, ctbuf, grecv, acts, curs,
    s_sem, s_rsem, p_sem, p_rsem, r_sem, r_rsem, d_sem, d_rsem, b_sem, b_rsem, f_sem, f_rsem,
    xr_sem, xr_rsem, xd_sem, xd_rsem, g_sem, g_rsem,
):
    pre, post, rep, chains, rh, n_pre = sizes
    ppp = pre // post
    rows = post * rh
    i, j, c = lax.axis_index("pre"), lax.axis_index("post"), lax.axis_index("rep")
    a_me = lax.rem(i, ppp)
    j_me = lax.div(i, ppp)
    home = j_me == j
    away = jnp.logical_not(home)
    group = pre * post * rep
    me = (i * post + j) * rep + c

    def where_is(flat):
        return {
            "pre": lax.div(flat, post * rep),
            "post": lax.rem(lax.div(flat, rep), post),
            "rep": lax.rem(flat, rep),
        }

    def peer(n):
        return lax.rem(me + n, group)

    barrier = pltpu.get_barrier_semaphore()

    def greet(n, carry):
        pl.semaphore_signal(barrier, inc=1, device_id=where_is(peer(n)), device_id_type=MESH)
        return carry

    lax.fori_loop(1, group, greet, 0)

    def copy(src, dst, send, recv, to):
        return pltpu.make_async_remote_copy(
            src_ref=src, dst_ref=dst, send_sem=send, recv_sem=recv, device_id=to, device_id_type=MESH
        )

    def flat_rows(value, lead):
        if rh % 16 == 0:
            return value.reshape(lead * rh, value.shape[-1])
        value = value.astype(F32)
        return value.reshape(lead * rh, value.shape[-1]).astype(BF16)

    mine = pl.ds(pl.multiple_of(a_me * n_pre, n_pre), n_pre)
    for which, ref in enumerate((stim_ref, cot_ref)):
        value = ref[:, mine].astype(F32)
        for ch in range(chains):
            for h in range(post):
                top = ch * rows + h * rh
                stage[which, ch, h] = value[top:top + rh].astype(BF16)
    ctsend[...] = jnp.broadcast_to(ct_ref[:, mine], ctsend.shape)
    start_rates = rates_ref[...].astype(F32)
    for ch in range(chains):
        for h in range(post):
            top = ch * rows + h * rh
            rbuf[0, 0, ch, h] = start_rates[top:top + rh].astype(BF16)

    pl.semaphore_wait(barrier, group - 1)

    def share_copies(h):
        to = {"post": h}
        yield copy(stage.at[0, :, h], sbuf.at[0], s_sem.at[h, 0], s_rsem.at[0], to)
        yield copy(stage.at[1, :, h], sbuf.at[1], s_sem.at[h, 1], s_rsem.at[1], to)
        yield copy(ctsend, ctbuf, s_sem.at[h, 2], s_rsem.at[2], to)

    for h in range(post):
        @pl.when(jnp.logical_and(home, h != j))
        def _():
            for one in share_copies(h):
                one.start()

    @pl.when(home)
    def _():
        for which in range(2):
            for ch in range(chains):
                sbuf[which, ch] = stage[which, ch, j]
        ctbuf[...] = ctsend[...]

    other = {"rep": 1 - c}

    def swap_rates(t, ch):
        return copy(rbuf.at[0, t, ch], rbuf.at[1, t, ch], xr_sem.at[t, ch], xr_rsem.at[t, ch], other)

    def swap_delta(t, ch, a):
        return copy(
            dbuf.at[0, a, t, ch], dbuf.at[1, a, t, ch], xd_sem.at[t, ch, a], xd_rsem.at[t, ch, a], other
        )

    def part_copy(t, ch, a, h):
        return copy(
            psend.at[t, ch, a, h], precv.at[t, ch, i], p_sem.at[t, ch, a, h], p_rsem.at[t, ch, i],
            {"pre": ppp * j + a, "post": h},
        )

    def is_me(m, h):
        return jnp.logical_and(m == i, h == j)

    def rate_copy(t, ch, d):
        return copy(
            rbuf.at[0, t, ch, j], rbuf.at[0, t, ch, j], r_sem.at[t, ch, d], r_rsem.at[t, ch, j],
            {"post": lax.rem(j + d, post)},
        )

    def delta_copy(t, ch, to_i):
        return copy(
            dsend.at[t, ch], dbuf.at[0, a_me, t, ch, j], d_sem.at[t, ch, to_i], d_rsem.at[t, ch, a_me, j],
            {"pre": to_i, "post": j_me},
        )

    def final_copy(ch, to_i):
        return copy(
            fbuf.at[1, ch, 0, 0], fbuf.at[0, ch, a_me, j], f_sem.at[ch, to_i], f_rsem.at[ch, a_me, j],
            {"pre": to_i, "post": j_me},
        )

    def back_copy(t, ch, d):
        h = lax.rem(j + d, post)
        return copy(
            bsend.at[t, ch, h], brecv.at[t, ch, j], b_sem.at[t, ch, d], b_rsem.at[t, ch, j], {"post": h}
        )

    def wait_slot(ref, sem):
        copy(ref, ref, sem, sem, other).wait_recv()

    gain = None
    for t in range(STEPS):
        for ch in range(chains):
            if t > 0:
                for d in range(1, post):
                    h = lax.rem(j + d, post)
                    wait_slot(rbuf.at[0, t, ch, h], r_rsem.at[t, ch, h])
            now = flat_rows(rbuf[0, t, ch], post)
            for a in range(ppp):
                part = jnp.dot(now, w_ref[:, a * n_pre:(a + 1) * n_pre], preferred_element_type=F32)
                for h in range(post):
                    psend[t, ch, a, h] = part[h * rh:(h + 1) * rh].astype(BF16)
                for h in range(post):
                    self_here = is_me(ppp * j + a, h)

                    @pl.when(jnp.logical_not(self_here))
                    def _():
                        part_copy(t, ch, a, h).start()

                    @pl.when(self_here)
                    def _():
                        precv[t, ch, i] = psend[t, ch, a, h]

            swap_rates(t, ch).start()
        if t == 0:
            @pl.when(away)
            def _():
                wait_slot(sbuf.at[0], s_rsem.at[0])
                wait_slot(sbuf.at[1], s_rsem.at[1])
                wait_slot(ctbuf, s_rsem.at[2])

            types = ctbuf[...]
            gain = jnp.zeros(types.shape, F32)
            for k in range(gains_ref.shape[0]):
                gain = jnp.where(types == k, gains_ref[k], gain)
            gain = gain[0:1]
        for ch in range(chains):
            cur = None
            for m in range(pre):
                remote = jnp.logical_or(away, m != i)

                @pl.when(remote)
                def _():
                    wait_slot(precv.at[t, ch, m], p_rsem.at[t, ch, m])

                term = precv[t, ch, m].astype(F32)
                cur = term if cur is None else cur + term
            act = jnp.tanh(gain * cur + sbuf[0, ch].astype(F32))
            acts[t, ch] = act
            curs[t, ch] = cur
            fresh = ((1.0 - LEAK) * rbuf[0, t, ch, j].astype(F32) + LEAK * act).astype(BF16)
            if t < STEPS - 1:
                rbuf[0, t + 1, ch, j] = fresh
                for d in range(1, post):
                    rate_copy(t + 1, ch, d).start()
            else:
                fbuf[1, ch, 0, 0] = fresh

    errors = [sbuf[1, ch].astype(F32) for ch in range(chains)]
    tally = jnp.zeros((8, n_pre), F32)
    for t in reversed(range(STEPS)):
        for ch in range(chains):
            error = errors[ch]
            if t < STEPS - 1:
                total = bsend[t + 1, ch, j].astype(F32)
                for d in range(1, post):
                    h = lax.rem(j + d, post)
                    wait_slot(brecv.at[t + 1, ch, h], b_rsem.at[t + 1, ch, h])
                    total = total + brecv[t + 1, ch, h].astype(F32)
                error = (1.0 - LEAK) * error + total
            errors[ch] = error
            act = acts[t, ch]
            du = error * LEAK * (1.0 - act * act)
            dsend[t, ch] = (du * gain).astype(BF16)
            for m in range(pre):
                remote = jnp.logical_or(away, m != i)

                @pl.when(remote)
                def _():
                    delta_copy(t, ch, m).start()

            @pl.when(home)
            def _():
                dbuf[0, a_me, t, ch, j] = dsend[t, ch]

            weighed = du * curs[t, ch]
            for top in range(0, rh, 8):
                tally = tally + weighed[top:top + 8]
        if t == 0:
            break
        for ch in range(chains):
            for a in range(ppp):
                for h in range(post):
                    @pl.when(jnp.logical_not(is_me(ppp * j + a, h)))
                    def _():
                        wait_slot(dbuf.at[0, a, t, ch, h], d_rsem.at[t, ch, a, h])

            back = None
            for a in range(ppp):
                term = lax.dot_general(
                    flat_rows(dbuf[0, a, t, ch], post), w_ref[:, a * n_pre:(a + 1) * n_pre],
                    (((1,), (1,)), ((), ())), preferred_element_type=F32,
                )
                back = term if back is None else back + term
            for h in range(post):
                bsend[t, ch, h] = back[h * rh:(h + 1) * rh].astype(BF16)
            for d in range(1, post):
                back_copy(t, ch, d).start()
            for a in range(ppp):
                swap_delta(t, ch, a).start()

    kinds = grecv.shape[-1]
    hot = (lax.broadcasted_iota(jnp.int32, (kinds, n_pre), 0) == ctbuf[0:1]).astype(F32)
    grecv[me] = lax.dot_general(
        tally, hot, (((1,), (1,)), ((), ())), preferred_element_type=F32, precision=lax.Precision.HIGHEST
    )

    def gain_copy(n):
        return copy(grecv.at[me], grecv.at[me], g_sem.at[n], g_rsem.at[me], where_is(peer(n)))

    def send_gain(n, carry):
        gain_copy(n).start()
        return carry

    lax.fori_loop(1, group, send_gain, 0)

    for ch in range(chains):
        for m in range(pre):
            @pl.when(jnp.logical_or(away, m != i))
            def _():
                final_copy(ch, m).start()

        @pl.when(home)
        def _():
            fbuf[0, ch, a_me, j] = fbuf[1, ch, 0, 0]

    for t in range(1, STEPS):
        for ch in range(chains):
            swap_rates(t, ch).wait_recv()
            for a in range(ppp):
                swap_delta(t, ch, a).wait_recv()
    for ch in range(chains):
        swap_rates(0, ch).wait_recv()

    def outer(side, low, high, a):
        lead = (high - low) * chains * post
        return lax.dot_general(
            flat_rows(rbuf[side, low:high], lead), flat_rows(dbuf[side, a, low:high], lead),
            (((0,), (0,)), ((), ())), preferred_element_type=F32,
        )

    for a in range(ppp):
        cols = slice(a * n_pre, (a + 1) * n_pre)
        g_ref[:, cols] = outer(0, 1, STEPS, a) + outer(1, 1, STEPS, a)
    for ch in range(chains):
        for a in range(ppp):
            for h in range(post):
                @pl.when(jnp.logical_not(is_me(ppp * j + a, h)))
                def _():
                    wait_slot(dbuf.at[0, a, 0, ch, h], d_rsem.at[0, ch, a, h])

            swap_delta(0, ch, a).start()
    for a in range(ppp):
        cols = slice(a * n_pre, (a + 1) * n_pre)
        for ch in range(chains):
            swap_delta(0, ch, a).wait_recv()
        g_ref[:, cols] += outer(0, 0, 1, a) + outer(1, 0, 1, a)

    for ch in range(chains):
        for a in range(ppp):
            for h in range(post):
                @pl.when(jnp.logical_not(is_me(ppp * j + a, h)))
                def _():
                    wait_slot(fbuf.at[0, ch, a, h], f_rsem.at[ch, a, h])

            final_ref[ch * rows:(ch + 1) * rows, a * n_pre:(a + 1) * n_pre] = flat_rows(fbuf[0, ch, a], post)

    def take_gain(n, carry):
        source = peer(n)
        wait_slot(grecv.at[source], g_rsem.at[source])
        return carry

    lax.fori_loop(1, group, take_gain, 0)
    gathered = grecv[0]
    for n in range(1, group):
        gathered = gathered + grecv[n]
    gg_ref[...] = jnp.sum(gathered, axis=0, keepdims=True)

    for h in range(post):
        @pl.when(jnp.logical_and(home, h != j))
        def _():
            for one in share_copies(h):
                one.wait_send()

    for t in range(STEPS):
        for ch in range(chains):
            swap_rates(t, ch).wait_send()
            for a in range(ppp):
                swap_delta(t, ch, a).wait_send()
                for h in range(post):
                    @pl.when(jnp.logical_not(is_me(ppp * j + a, h)))
                    def _():
                        part_copy(t, ch, a, h).wait_send()

            for m in range(pre):
                @pl.when(jnp.logical_or(away, m != i))
                def _():
                    delta_copy(t, ch, m).wait_send()
                    if t == 0:
                        final_copy(ch, m).wait_send()

            if t > 0:
                for d in range(1, post):
                    rate_copy(t, ch, d).wait_send()
                    back_copy(t, ch, d).wait_send()

    def end_gain(n, carry):
        gain_copy(n).wait_send()
        return carry

    lax.fori_loop(1, group, end_gain, 0)


def body(rates0, stimulus, cotangent, weights, src_block, dst_block, live_count, cell_type, gains):
    pre, post, rep = lax.axis_size("pre"), lax.axis_size("post"), lax.axis_size("rep")
    batch, n_pre = rates0.shape
    n_post = stimulus.shape[1]
    slots, width = weights.shape[2], weights.shape[3]
    ppp = pre // post
    chains = 2 if batch // (2 * post) >= 16 else 1
    rh = batch // (chains * post)
    group = pre * post * rep
    smem = pl.BlockSpec(memory_space=pltpu.SMEM)
    vmem = pl.BlockSpec(memory_space=pltpu.VMEM)

    dense = pl.pallas_call(
        build_kernel,
        grid=(slots // CHUNK,),
        out_shape=jax.ShapeDtypeStruct((n_pre, n_post), BF16),
        in_specs=[smem, smem, smem, pl.BlockSpec((1, 1, CHUNK, width, width), lambda p: (0, 0, p, 0, 0))],
        out_specs=pl.BlockSpec((n_pre, n_post), lambda p: (0, 0)),
        scratch_shapes=[pltpu.VMEM((n_pre, n_post), F32)],
        compiler_params=pltpu.CompilerParams(vmem_limit_bytes=32 * 2**20),
        name="dense_tile",
    )(src_block, dst_block, live_count, weights)

    dma = pltpu.SemaphoreType.DMA
    V = pltpu.VMEM
    final, gain_grad, dense_grad = pl.pallas_call(
        functools.partial(step_kernel, (pre, post, rep, chains, rh, n_pre)),
        out_shape=(
            jax.ShapeDtypeStruct((batch, n_post), BF16),
            jax.ShapeDtypeStruct((1, 128), F32),
            jax.ShapeDtypeStruct((n_pre, n_post), F32),
        ),
        in_specs=[vmem, vmem, vmem, vmem, vmem, smem],
        out_specs=(vmem, vmem, vmem),
        scratch_shapes=[
            V((2, STEPS, chains, post, rh, n_pre), BF16),
            V((2, ppp, STEPS, chains, post, rh, n_pre), BF16),
            V((2, chains, ppp, post, rh, n_pre), BF16),
            V((STEPS, chains, ppp, post, rh, n_pre), BF16),
            V((STEPS, chains, pre, rh, n_pre), BF16),
            V((STEPS, chains, rh, n_pre), BF16),
            V((STEPS, chains, post, rh, n_pre), BF16),
            V((STEPS, chains, post, rh, n_pre), BF16),
            V((2, chains, post, rh, n_pre), BF16),
            V((2, chains, rh, n_pre), BF16),
            V((8, n_pre), jnp.int32),
            V((8, n_pre), jnp.int32),
            V((group, 8, 128), F32),
            V((STEPS, chains, rh, n_pre), F32),
            V((STEPS, chains, rh, n_pre), F32),
            dma((post, 3)), dma((3,)),
            dma((STEPS, chains, ppp, post)), dma((STEPS, chains, pre)),
            dma((STEPS, chains, post)), dma((STEPS, chains, post)),
            dma((STEPS, chains, pre)), dma((STEPS, chains, ppp, post)),
            dma((STEPS, chains, post)), dma((STEPS, chains, post)),
            dma((chains, pre)), dma((chains, ppp, post)),
            dma((STEPS, chains)), dma((STEPS, chains)),
            dma((STEPS, chains, ppp)), dma((STEPS, chains, ppp)),
            dma((group,)), dma((group,)),
        ],
        compiler_params=pltpu.CompilerParams(
            collective_id=0, has_side_effects=True, vmem_limit_bytes=48 * 2**20
        ),
        name="window",
    )(rates0, stimulus, cotangent, dense, cell_type.reshape(1, n_post), gains)

    share = slots // rep
    grad = pl.pallas_call(
        emit_kernel,
        out_shape=jax.ShapeDtypeStruct((1, 1, share, width, width), F32),
        in_specs=[smem, smem, smem, vmem],
        out_specs=pl.BlockSpec(memory_space=pl.ANY),
        scratch_shapes=[V((width, width), F32), dma((share,))],
        compiler_params=pltpu.CompilerParams(vmem_limit_bytes=32 * 2**20),
        name="emit_slots",
    )(src_block, dst_block, live_count, dense_grad)
    return final, grad, gain_grad[0, :gains.shape[0]]


def solution(mesh):
    return jax.shard_map(
        body,
        mesh=mesh,
        in_specs=(
            P(("groups", "rep"), "pre"),
            P(("groups", "rep"), "post"),
            P(("groups", "rep"), "post"),
            P(("groups", "pre"), "post", None, None, None),
            P(("groups", "pre"), "post", None),
            P(("groups", "pre"), "post", None),
            P(("groups", "pre"), "post"),
            P(("groups", "post")),
            P(),
        ),
        out_specs=(
            P(("groups", "rep"), "post"),
            P(("groups", "pre"), "post", "rep", None, None),
            P("groups"),
        ),
        check_vma=False,
    )
```

```python
import functools

import jax
import jax.numpy as jnp
from jax import lax
from jax.experimental import pallas as pl
from jax.experimental.pallas import tpu as pltpu
from jax.sharding import PartitionSpec as P

STEPS = 4
LEAK = 0.35
MESH = pl.DeviceIdType.MESH
F32 = jnp.float32
BF16 = jnp.bfloat16
CHUNK = 8


def build_kernel(src_ref, dst_ref, live_ref, w_ref, out_ref, acc):
    width = w_ref.shape[-1]
    part = pl.program_id(0)

    @pl.when(part == 0)
    def _():
        acc[...] = jnp.zeros_like(acc)

    live = live_ref[0, 0]
    for s in range(CHUNK):
        k = part * CHUNK + s

        @pl.when(k < live)
        def _():
            rows = pl.ds(pl.multiple_of(src_ref[0, 0, k] * width, width), width)
            block = dst_ref[0, 0, k]
            across = acc.shape[2] // width
            cols = pl.ds(pl.multiple_of(lax.rem(block, across) * width, width), width)
            acc[lax.div(block, across), rows, cols] += w_ref[0, 0, s].astype(F32)

    @pl.when(part == pl.num_programs(0) - 1)
    def _():
        out_ref[...] = acc[...].astype(BF16)


def emit_kernel(src_ref, dst_ref, live_ref, g_ref, out_ref, zero, sem):
    width = zero.shape[0]
    share = out_ref.shape[2]
    first = lax.axis_index("rep") * share
    live = live_ref[0, 0]
    zero[...] = jnp.zeros_like(zero)

    def start(k, carry):
        slot = first + k

        @pl.when(slot < live)
        def _():
            rows = pl.ds(pl.multiple_of(src_ref[0, 0, slot] * width, width), width)
            cols = pl.ds(pl.multiple_of(dst_ref[0, 0, slot] * width, width), width)
            pltpu.make_async_copy(g_ref.at[rows, cols], out_ref.at[0, 0, k], sem.at[k]).start()

        @pl.when(slot >= live)
        def _():
            pltpu.make_async_copy(zero, out_ref.at[0, 0, k], sem.at[k]).start()

        return carry

    lax.fori_loop(0, share, start, 0)

    def finish(k, carry):
        pltpu.make_async_copy(zero, out_ref.at[0, 0, k], sem.at[k]).wait()
        return carry

    lax.fori_loop(0, share, finish, 0)


def step_kernel(
    sizes,
    rates_ref, stim_ref, cot_ref, w_ref, ct_ref, gains_ref,
    final_ref, gg_ref, g_ref,
    wbuf, rbuf, dbuf, dz, fbuf, psend, precv, dsend, stage, sbuf, ctsend, ctbuf, grecv, acts, curs,
    w_sem, w_rsem, wx_sem, wx_rsem,
    s_sem, s_rsem, p_sem, p_rsem, r_sem, r_rsem, z_sem, z_rsem, q_sem, q_rsem, d_sem, d_rsem, f_sem, f_rsem,
    xd_sem, xd_rsem, g_sem, g_rsem,
):
    pre, post, rep, chains, rh, n_pre = sizes
    ppp = pre // post
    rows = chains * rh
    i, j, c = lax.axis_index("pre"), lax.axis_index("post"), lax.axis_index("rep")
    a_me = lax.rem(i, ppp)
    j_me = lax.div(i, ppp)
    home = j_me == j
    away = jnp.logical_not(home)
    group = pre * post * rep
    me = (i * post + j) * rep + c

    def where_is(flat):
        return {
            "pre": lax.div(flat, post * rep),
            "post": lax.rem(lax.div(flat, rep), post),
            "rep": lax.rem(flat, rep),
        }

    def peer(n):
        return lax.rem(me + n, group)

    barrier = pltpu.get_barrier_semaphore()

    def greet(n, carry):
        pl.semaphore_signal(barrier, inc=1, device_id=where_is(peer(n)), device_id_type=MESH)
        return carry

    lax.fori_loop(1, group, greet, 0)

    def copy(src, dst, send, recv, to):
        return pltpu.make_async_remote_copy(
            src_ref=src, dst_ref=dst, send_sem=send, recv_sem=recv, device_id=to, device_id_type=MESH
        )

    def flat_rows(value, lead):
        if rh % 16 == 0:
            return value.reshape(lead * rh, value.shape[-1])
        value = value.astype(F32)
        return value.reshape(lead * rh, value.shape[-1]).astype(BF16)

    def one_block(value):
        return value

    mine = pl.ds(pl.multiple_of(a_me * n_pre, n_pre), n_pre)
    for which, ref in enumerate((stim_ref, cot_ref)):
        value = ref[:, mine].astype(F32)
        for ch in range(chains):
            for h in range(post):
                top = h * rows + ch * rh
                stage[which, h, ch] = value[top:top + rh].astype(BF16)
    ctsend[...] = jnp.broadcast_to(ct_ref[:, mine], ctsend.shape)
    start_rates = rates_ref[...].astype(F32)
    for h in range(post):
        @pl.when(h == j)
        def _():
            for ch in range(chains):
                top = h * rows + ch * rh
                rbuf[0, 0, ch, h] = start_rates[top:top + rh].astype(BF16)

    half = n_pre // rep
    band = pl.ds(pl.multiple_of(c * half, half), half)
    other = {"rep": 1 - c}

    def weight_copy(d, a):
        to = {"post": lax.rem(j + d, post)}
        slot = j * ppp + a
        return copy(w_ref.at[a, band], wbuf.at[slot, band], w_sem.at[d, a], w_rsem.at[slot], to)

    def weight_swap(h, a):
        slot = h * ppp + a
        there = wbuf.at[slot, band]
        return copy(there, there, wx_sem.at[slot], wx_rsem.at[slot], other)

    pl.semaphore_wait(barrier, group - 1)

    def share_copies(h):
        to = {"post": h}
        yield copy(stage.at[0, h], sbuf.at[0], s_sem.at[h, 0], s_rsem.at[0], to)
        yield copy(stage.at[1, h], sbuf.at[1], s_sem.at[h, 1], s_rsem.at[1], to)
        yield copy(ctsend, ctbuf, s_sem.at[h, 2], s_rsem.at[2], to)

    for h in range(post):
        @pl.when(jnp.logical_and(home, h != j))
        def _():
            for one in share_copies(h):
                one.start()

    @pl.when(home)
    def _():
        for which in range(2):
            for ch in range(chains):
                sbuf[which, ch] = stage[which, j, ch]
        ctbuf[...] = ctsend[...]


    def swap_delta(t, ch, a):
        return copy(
            dbuf.at[0, a, t, ch], dbuf.at[1, a, t, ch], xd_sem.at[ch, a], xd_rsem.at[ch, a], other
        )

    def part_copy(t, ch, m):
        return copy(
            psend.at[t, ch, m], precv.at[t, ch, i], p_sem.at[t, ch, m], p_rsem.at[t, ch, i], {"pre": m}
        )

    def first_copy(ch, a, h):
        return copy(
            psend.at[0, ch, a * post + h], precv.at[0, ch, i], p_sem.at[0, ch, a * post + h],
            p_rsem.at[0, ch, i], {"pre": ppp * j + a, "post": h},
        )

    def cross(n):
        return lax.rem(j + n // rep, post), n % rep

    def spread_rates(t, ch, n):
        h, side = cross(n)
        to = {"post": h, "rep": lax.rem(c + side, rep)}
        return copy(
            rbuf.at[0, t, ch, j], rbuf.at[side, t, ch, j], r_sem.at[t, ch, n], r_rsem.at[side, t, ch, j], to
        )

    def spread_delta(t, ch, a, n):
        h, side = cross(n)
        to = {"post": h, "rep": lax.rem(c + side, rep)}
        return copy(
            dz.at[t, ch, h * ppp + a], dbuf.at[side, a, t, ch, j], q_sem.at[t, ch, a, n],
            q_rsem.at[side, a, t, ch, j], to,
        )

    def gather_copy(t, ch, d):
        return copy(
            dz.at[t, ch, i], dz.at[t, ch, i], z_sem.at[t, ch, d], z_rsem.at[t, ch, i],
            {"pre": lax.rem(i + d, pre)},
        )

    def is_me(m, h):
        return jnp.logical_and(m == i, h == j)

    def delta_copy(t, ch, to_i):
        return copy(
            dsend.at[ch], dbuf.at[0, a_me, t, ch, j], d_sem.at[ch, to_i], d_rsem.at[ch, a_me, j],
            {"pre": to_i, "post": j_me},
        )

    def final_copy(ch, to_i):
        return copy(
            fbuf.at[1, 0, 0, ch], fbuf.at[0, a_me, j, ch], f_sem.at[ch, to_i], f_rsem.at[ch, a_me, j],
            {"pre": to_i, "post": j_me},
        )

    def wait_slot(ref, sem):
        copy(ref, ref, sem, sem, other).wait_recv()

    gain = None
    def send_part(t, ch, m, now):
        psend[t, ch, m] = jnp.dot(now, wbuf[m], preferred_element_type=F32).astype(BF16)
        part_copy(t, ch, m).start()

    def own_part(t, ch, now):
        precv[t, ch, i] = jnp.dot(now, wbuf[i], preferred_element_type=F32).astype(BF16)

    reach = [d for d in range(2, pre)] + [1]
    for t in range(STEPS):
        if t == 0:
            for a in range(ppp):
                part = jnp.dot(rates_ref[...], w_ref[a], preferred_element_type=F32)
                for h in range(post):
                    for ch in range(chains):
                        top = h * rows + ch * rh
                        value = part[top:top + rh].astype(BF16)
                        here = is_me(ppp * j + a, h)

                        @pl.when(here)
                        def _():
                            precv[0, ch, i] = value

                        @pl.when(jnp.logical_not(here))
                        def _():
                            psend[0, ch, a * post + h] = value
                            first_copy(ch, a, h).start()

            for d in range(1, post):
                for a in range(ppp):
                    weight_copy(d, a).start()
            for a in range(ppp):
                wbuf[j * ppp + a] = w_ref[a]
        elif t == 1:
            nexts = [one_block(rbuf[0, 1, ch, j]) for ch in range(chains)]
            for d in range(post):
                h = lax.rem(j + d, post)
                if d > 0:
                    for a in range(ppp):
                        wait_slot(wbuf.at[h * ppp + a, band], w_rsem.at[h * ppp + a])
                        weight_swap(h, a).start()
                for a in range(ppp):
                    m = h * ppp + a
                    if d > 0:
                        wait_slot(wbuf.at[m, band], wx_rsem.at[m])
                    for ch in range(chains):
                        @pl.when(m != i)
                        def _():
                            send_part(1, ch, m, nexts[ch])

                        @pl.when(m == i)
                        def _():
                            own_part(1, ch, nexts[ch])

        for ch in range(chains):
            if t > 1:
                now = one_block(rbuf[0, t, ch, j])
                for d in reach:
                    send_part(t, ch, lax.rem(i + d, pre), now)
                own_part(t, ch, now)
            for n in range(1, post * rep):
                spread_rates(t, ch, n).start()
        if t == 0:
            @pl.when(away)
            def _():
                wait_slot(sbuf.at[0], s_rsem.at[0])
                wait_slot(sbuf.at[1], s_rsem.at[1])
                wait_slot(ctbuf, s_rsem.at[2])

            types = ctbuf[...]
            gain = jnp.zeros(types.shape, F32)
            for k in range(gains_ref.shape[0]):
                gain = jnp.where(types == k, gains_ref[k], gain)
            gain = gain[0:1]
        for ch in range(chains):
            if t == 0:
                for m in range(pre):
                    @pl.when(jnp.logical_or(away, m != i))
                    def _():
                        wait_slot(precv.at[0, ch, m], p_rsem.at[0, ch, m])

            else:
                for d in range(1, pre):
                    m = lax.rem(i + d, pre)
                    wait_slot(precv.at[t, ch, m], p_rsem.at[t, ch, m])
            cur = precv[t, ch, 0].astype(F32)
            for m in range(1, pre):
                cur = cur + precv[t, ch, m].astype(F32)
            act = jnp.tanh(gain * cur + sbuf[0, ch].astype(F32))
            acts[t, ch] = act
            curs[t, ch] = cur
            fresh = ((1.0 - LEAK) * rbuf[0, t, ch, j].astype(F32) + LEAK * act).astype(BF16)
            if t < STEPS - 1:
                rbuf[0, t + 1, ch, j] = fresh
            else:
                fbuf[1, 0, 0, ch] = fresh

    errors = [sbuf[1, ch].astype(F32) for ch in range(chains)]
    tally = jnp.zeros((8, n_pre), F32)
    for t in reversed(range(STEPS)):
        for ch in range(chains):
            error = errors[ch]
            act = acts[t, ch]
            du = error * LEAK * (1.0 - act * act)
            delta = (du * gain).astype(BF16)
            if t > 0:
                dz[t, ch, i] = delta
                for d in reach:
                    gather_copy(t, ch, d).start()
            else:
                dsend[ch] = delta
                for m in range(pre):
                    @pl.when(jnp.logical_or(away, m != i))
                    def _():
                        delta_copy(0, ch, m).start()

                @pl.when(home)
                def _():
                    dbuf[0, a_me, 0, ch, j] = dsend[ch]

            weighed = du * curs[t, ch]
            for top in range(0, rh, 8):
                tally = tally + weighed[top:top + 8]
        if t == 0:
            break
        for ch in range(chains):
            back = None
            for d in range(pre):
                m = lax.rem(i + d, pre)
                if d > 0:
                    wait_slot(dz.at[t, ch, m], z_rsem.at[t, ch, m])
                term = lax.dot_general(
                    one_block(dz[t, ch, m]), wbuf[m], (((1,), (1,)), ((), ())), preferred_element_type=F32
                )
                back = term if back is None else back + term
            errors[ch] = (1.0 - LEAK) * errors[ch] + back
            for a in range(ppp):
                for n in range(1, post * rep):
                    spread_delta(t, ch, a, n).start()
                dbuf[0, a, t, ch, j] = dz[t, ch, j * ppp + a]

    kinds = grecv.shape[-1]
    hot = (lax.broadcasted_iota(jnp.int32, (kinds, n_pre), 0) == ctbuf[0:1]).astype(F32)
    grecv[me] = lax.dot_general(
        tally, hot, (((1,), (1,)), ((), ())), preferred_element_type=F32, precision=lax.Precision.HIGHEST
    )

    def gain_copy(n):
        return copy(grecv.at[me], grecv.at[me], g_sem.at[n], g_rsem.at[me], where_is(peer(n)))

    def send_gain(n, carry):
        gain_copy(n).start()
        return carry

    lax.fori_loop(1, group, send_gain, 0)

    for ch in range(chains):
        for m in range(pre):
            @pl.when(jnp.logical_or(away, m != i))
            def _():
                final_copy(ch, m).start()

        @pl.when(home)
        def _():
            fbuf[0, a_me, j, ch] = fbuf[1, 0, 0, ch]

    for t in range(STEPS):
        for ch in range(chains):
            for n in range(1, post * rep):
                h, side = cross(n)
                wait_slot(rbuf.at[side, t, ch, h], r_rsem.at[side, t, ch, h])
                if t > 0:
                    for a in range(ppp):
                        wait_slot(dbuf.at[side, a, t, ch, h], q_rsem.at[side, a, t, ch, h])

    def outer(side, low, high, a):
        lead = (high - low) * chains * post
        return lax.dot_general(
            flat_rows(rbuf[side, low:high], lead), flat_rows(dbuf[side, a, low:high], lead),
            (((0,), (0,)), ((), ())), preferred_element_type=F32,
        )

    for a in range(ppp):
        cols = slice(a * n_pre, (a + 1) * n_pre)
        g_ref[:, cols] = outer(0, 1, STEPS, a) + outer(1, 1, STEPS, a)
    for ch in range(chains):
        for a in range(ppp):
            for h in range(post):
                @pl.when(jnp.logical_not(is_me(ppp * j + a, h)))
                def _():
                    wait_slot(dbuf.at[0, a, 0, ch, h], d_rsem.at[ch, a, h])

            swap_delta(0, ch, a).start()
    for a in range(ppp):
        cols = slice(a * n_pre, (a + 1) * n_pre)
        for ch in range(chains):
            swap_delta(0, ch, a).wait_recv()
        g_ref[:, cols] += outer(0, 0, 1, a) + outer(1, 0, 1, a)

    for a in range(ppp):
        for h in range(post):
            for ch in range(chains):
                @pl.when(jnp.logical_not(is_me(ppp * j + a, h)))
                def _():
                    wait_slot(fbuf.at[0, a, h, ch], f_rsem.at[ch, a, h])

        final_ref[:, a * n_pre:(a + 1) * n_pre] = flat_rows(fbuf[0, a], post * chains)

    def take_gain(n, carry):
        source = peer(n)
        wait_slot(grecv.at[source], g_rsem.at[source])
        return carry

    lax.fori_loop(1, group, take_gain, 0)
    gathered = grecv[0]
    for n in range(1, group):
        gathered = gathered + grecv[n]
    gg_ref[...] = jnp.sum(gathered, axis=0, keepdims=True)[:, :gg_ref.shape[1]]

    for h in range(post):
        @pl.when(jnp.logical_and(home, h != j))
        def _():
            for one in share_copies(h):
                one.wait_send()

    for d in range(1, post):
        h = lax.rem(j + d, post)
        for a in range(ppp):
            weight_copy(d, a).wait_send()
            weight_swap(h, a).wait_send()
    for t in range(STEPS):
        for ch in range(chains):
            for d in reach:
                if t > 0:
                    part_copy(t, ch, lax.rem(i + d, pre)).wait_send()
                    gather_copy(t, ch, d).wait_send()
            for n in range(1, post * rep):
                spread_rates(t, ch, n).wait_send()
                if t > 0:
                    for a in range(ppp):
                        spread_delta(t, ch, a, n).wait_send()
    for ch in range(chains):
        for a in range(ppp):
            swap_delta(0, ch, a).wait_send()
            for h in range(post):
                @pl.when(jnp.logical_not(is_me(ppp * j + a, h)))
                def _():
                    first_copy(ch, a, h).wait_send()

        for m in range(pre):
            @pl.when(jnp.logical_or(away, m != i))
            def _():
                delta_copy(0, ch, m).wait_send()
                final_copy(ch, m).wait_send()

    def end_gain(n, carry):
        gain_copy(n).wait_send()
        return carry

    lax.fori_loop(1, group, end_gain, 0)


def body(rates0, stimulus, cotangent, weights, src_block, dst_block, live_count, cell_type, gains):
    pre, post, rep = lax.axis_size("pre"), lax.axis_size("post"), lax.axis_size("rep")
    batch, n_pre = rates0.shape
    n_post = stimulus.shape[1]
    slots, width = weights.shape[2], weights.shape[3]
    ppp = pre // post
    chains = 1
    rh = batch // (chains * post)
    group = pre * post * rep
    smem = pl.BlockSpec(memory_space=pltpu.SMEM)
    vmem = pl.BlockSpec(memory_space=pltpu.VMEM)

    dense = pl.pallas_call(
        build_kernel,
        grid=(slots // CHUNK,),
        out_shape=jax.ShapeDtypeStruct((ppp, n_pre, n_pre), BF16),
        in_specs=[smem, smem, smem, pl.BlockSpec((1, 1, CHUNK, width, width), lambda p: (0, 0, p, 0, 0))],
        out_specs=pl.BlockSpec((ppp, n_pre, n_pre), lambda p: (0, 0, 0)),
        scratch_shapes=[pltpu.VMEM((ppp, n_pre, n_pre), F32)],
        compiler_params=pltpu.CompilerParams(vmem_limit_bytes=32 * 2**20),
        name="dense_tile",
    )(src_block, dst_block, live_count, weights)

    dma = pltpu.SemaphoreType.DMA
    V = pltpu.VMEM
    final, gain_grad, dense_grad = pl.pallas_call(
        functools.partial(step_kernel, (pre, post, rep, chains, rh, n_pre)),
        out_shape=(
            jax.ShapeDtypeStruct((batch, n_post), BF16),
            jax.ShapeDtypeStruct((1, gains.shape[0]), F32),
            jax.ShapeDtypeStruct((n_pre, n_post), F32),
        ),
        in_specs=[vmem, vmem, vmem, vmem, vmem, smem],
        out_specs=(vmem, vmem, vmem),
        scratch_shapes=[
            V((pre, n_pre, n_pre), BF16),
            V((2, STEPS, chains, post, rh, n_pre), BF16),
            V((2, ppp, STEPS, chains, post, rh, n_pre), BF16),
            V((STEPS, chains, pre, rh, n_pre), BF16),
            V((2, ppp, post, chains, rh, n_pre), BF16),
            V((STEPS, chains, pre, rh, n_pre), BF16),
            V((STEPS, chains, pre, rh, n_pre), BF16),
            V((chains, rh, n_pre), BF16),
            V((2, post, chains, rh, n_pre), BF16),
            V((2, chains, rh, n_pre), BF16),
            V((8, n_pre), jnp.int32),
            V((8, n_pre), jnp.int32),
            V((group, 8, 128), F32),
            V((STEPS, chains, rh, n_pre), F32),
            V((STEPS, chains, rh, n_pre), F32),
            dma((post, ppp)), dma((pre,)), dma((pre,)), dma((pre,)),
            dma((post, 3)), dma((3,)),
            dma((STEPS, chains, pre)), dma((STEPS, chains, pre)),
            dma((STEPS, chains, post * rep)), dma((rep, STEPS, chains, post)),
            dma((STEPS, chains, pre)), dma((STEPS, chains, pre)),
            dma((STEPS, chains, ppp, post * rep)), dma((rep, ppp, STEPS, chains, post)),
            dma((chains, pre)), dma((chains, ppp, post)),
            dma((chains, pre)), dma((chains, ppp, post)),
            dma((chains, ppp)), dma((chains, ppp)),
            dma((group,)), dma((group,)),
        ],
        compiler_params=pltpu.CompilerParams(
            collective_id=0, has_side_effects=True, vmem_limit_bytes=48 * 2**20
        ),
        name="window",
    )(rates0, stimulus, cotangent, dense, cell_type.reshape(1, n_post), gains)

    share = slots // rep
    grad = pl.pallas_call(
        emit_kernel,
        out_shape=jax.ShapeDtypeStruct((1, 1, share, width, width), F32),
        in_specs=[smem, smem, smem, vmem],
        out_specs=pl.BlockSpec(memory_space=pl.ANY),
        scratch_shapes=[V((width, width), F32), dma((share,))],
        compiler_params=pltpu.CompilerParams(vmem_limit_bytes=32 * 2**20),
        name="emit_slots",
    )(src_block, dst_block, live_count, dense_grad)
    return final, grad, gain_grad.reshape(gains.shape)


def solution(mesh):
    return jax.shard_map(
        body,
        mesh=mesh,
        in_specs=(
            P(("groups", "rep"), "pre"),
            P(("groups", "rep"), "post"),
            P(("groups", "rep"), "post"),
            P(("groups", "pre"), "post", None, None, None),
            P(("groups", "pre"), "post", None),
            P(("groups", "pre"), "post", None),
            P(("groups", "pre"), "post"),
            P(("groups", "post")),
            P(),
        ),
        out_specs=(
            P(("groups", "rep"), "post"),
            P(("groups", "pre"), "post", "rep", None, None),
            P("groups"),
        ),
        check_vma=False,
    )
```

```python
import functools

import jax
import jax.numpy as jnp
from jax import lax
from jax.experimental import pallas as pl
from jax.experimental.pallas import tpu as pltpu
from jax.sharding import PartitionSpec as P

STEPS = 4
LEAK = 0.35
MESH = pl.DeviceIdType.MESH
F32 = jnp.float32
BF16 = jnp.bfloat16
CHUNK = 8


def build_kernel(src_ref, dst_ref, live_ref, w_ref, out_ref, acc):
    width = w_ref.shape[-1]
    part = pl.program_id(0)

    @pl.when(part == 0)
    def _():
        acc[...] = jnp.zeros_like(acc)

    live = live_ref[0, 0]
    for s in range(CHUNK):
        k = part * CHUNK + s

        @pl.when(k < live)
        def _():
            rows = pl.ds(pl.multiple_of(src_ref[0, 0, k] * width, width), width)
            block = dst_ref[0, 0, k]
            across = acc.shape[2] // width
            cols = pl.ds(pl.multiple_of(lax.rem(block, across) * width, width), width)
            acc[lax.div(block, across), rows, cols] += w_ref[0, 0, s].astype(F32)

    @pl.when(part == pl.num_programs(0) - 1)
    def _():
        out_ref[...] = acc[...].astype(BF16)


def emit_kernel(src_ref, dst_ref, live_ref, g_ref, out_ref, zero, sem):
    width = zero.shape[0]
    share = out_ref.shape[2]
    first = lax.axis_index("rep") * share
    live = live_ref[0, 0]
    zero[...] = jnp.zeros_like(zero)

    def start(k, carry):
        slot = first + k

        @pl.when(slot < live)
        def _():
            rows = pl.ds(pl.multiple_of(src_ref[0, 0, slot] * width, width), width)
            cols = pl.ds(pl.multiple_of(dst_ref[0, 0, slot] * width, width), width)
            pltpu.make_async_copy(g_ref.at[rows, cols], out_ref.at[0, 0, k], sem.at[k]).start()

        @pl.when(slot >= live)
        def _():
            pltpu.make_async_copy(zero, out_ref.at[0, 0, k], sem.at[k]).start()

        return carry

    lax.fori_loop(0, share, start, 0)

    def finish(k, carry):
        pltpu.make_async_copy(zero, out_ref.at[0, 0, k], sem.at[k]).wait()
        return carry

    lax.fori_loop(0, share, finish, 0)


def step_kernel(
    sizes,
    rates_ref, stim_ref, cot_ref, w_ref, ct_ref, gains_ref,
    final_ref, gg_ref, g_ref,
    wbuf, rbuf, dbuf, dz, fbuf, psend, precv, dsend, stage, sbuf, ctsend, ctbuf, grecv, acts, curs,
    w_sem, w_rsem, wx_sem, wx_rsem,
    s_sem, s_rsem, p_sem, p_rsem, r_sem, r_rsem, z_sem, z_rsem, q_sem, q_rsem, d_sem, d_rsem, f_sem, f_rsem,
    xd_sem, xd_rsem, g_sem, g_rsem,
):
    pre, post, rep, chains, rh, n_pre = sizes
    ppp = pre // post
    rows = chains * rh
    i, j, c = lax.axis_index("pre"), lax.axis_index("post"), lax.axis_index("rep")
    a_me = lax.rem(i, ppp)
    j_me = lax.div(i, ppp)
    home = j_me == j
    away = jnp.logical_not(home)
    group = pre * post * rep
    me = (i * post + j) * rep + c

    def where_is(flat):
        return {
            "pre": lax.div(flat, post * rep),
            "post": lax.rem(lax.div(flat, rep), post),
            "rep": lax.rem(flat, rep),
        }

    def peer(n):
        return lax.rem(me + n, group)

    barrier = pltpu.get_barrier_semaphore()

    def greet(n, carry):
        pl.semaphore_signal(barrier, inc=1, device_id=where_is(peer(n)), device_id_type=MESH)
        return carry

    lax.fori_loop(1, group, greet, 0)

    def copy(src, dst, send, recv, to):
        return pltpu.make_async_remote_copy(
            src_ref=src, dst_ref=dst, send_sem=send, recv_sem=recv, device_id=to, device_id_type=MESH
        )

    def flat_rows(value, lead):
        if rh % 16 == 0:
            return value.reshape(lead * rh, value.shape[-1])
        value = value.astype(F32)
        return value.reshape(lead * rh, value.shape[-1]).astype(BF16)

    def one_block(value):
        return value

    mine = pl.ds(pl.multiple_of(a_me * n_pre, n_pre), n_pre)
    for which, ref in enumerate((stim_ref, cot_ref)):
        value = ref[:, mine].astype(F32)
        for ch in range(chains):
            for h in range(post):
                top = h * rows + ch * rh
                stage[which, h, ch] = value[top:top + rh].astype(BF16)
    ctsend[...] = jnp.broadcast_to(ct_ref[:, mine], ctsend.shape)
    start_rates = rates_ref[...].astype(F32)
    for h in range(post):
        @pl.when(h == j)
        def _():
            for ch in range(chains):
                top = h * rows + ch * rh
                rbuf[0, 0, ch, h] = start_rates[top:top + rh].astype(BF16)

    half = n_pre // rep
    band = pl.ds(pl.multiple_of(c * half, half), half)
    other = {"rep": 1 - c}

    def weight_copy(d, a):
        to = {"post": lax.rem(j + d, post)}
        slot = j * ppp + a
        return copy(w_ref.at[a, band], wbuf.at[slot, band], w_sem.at[d, a], w_rsem.at[slot], to)

    def weight_swap(h, a):
        slot = h * ppp + a
        there = wbuf.at[slot, band]
        return copy(there, there, wx_sem.at[slot], wx_rsem.at[slot], other)

    pl.semaphore_wait(barrier, group - 1)

    for d in range(1, post):
        for a in range(ppp):
            weight_copy(d, a).start()

    def share_copies(h):
        to = {"post": h}
        yield copy(stage.at[0, h], sbuf.at[0], s_sem.at[h, 0], s_rsem.at[0], to)
        yield copy(stage.at[1, h], sbuf.at[1], s_sem.at[h, 1], s_rsem.at[1], to)
        yield copy(ctsend, ctbuf, s_sem.at[h, 2], s_rsem.at[2], to)

    for h in range(post):
        @pl.when(jnp.logical_and(home, h != j))
        def _():
            for one in share_copies(h):
                one.start()

    @pl.when(home)
    def _():
        for which in range(2):
            for ch in range(chains):
                sbuf[which, ch] = stage[which, j, ch]
        ctbuf[...] = ctsend[...]


    def swap_delta(t, ch, a):
        return copy(
            dbuf.at[0, a, t, ch], dbuf.at[1, a, t, ch], xd_sem.at[ch, a], xd_rsem.at[ch, a], other
        )

    def part_copy(t, ch, m):
        return copy(
            psend.at[t, ch, m], precv.at[t, ch, i], p_sem.at[t, ch, m], p_rsem.at[t, ch, i], {"pre": m}
        )

    def first_copy(ch, a, h):
        return copy(
            psend.at[0, ch, a * post + h], precv.at[0, ch, i], p_sem.at[0, ch, a * post + h],
            p_rsem.at[0, ch, i], {"pre": ppp * j + a, "post": h},
        )

    def cross(n):
        return lax.rem(j + n // rep, post), n % rep

    def spread_rates(t, ch, n):
        h, side = cross(n)
        to = {"post": h, "rep": lax.rem(c + side, rep)}
        return copy(
            rbuf.at[0, t, ch, j], rbuf.at[side, t, ch, j], r_sem.at[t, ch, n], r_rsem.at[side, t, ch, j], to
        )

    def spread_delta(t, ch, a, n):
        h, side = cross(n)
        to = {"post": h, "rep": lax.rem(c + side, rep)}
        return copy(
            dz.at[t, ch, h * ppp + a], dbuf.at[side, a, t, ch, j], q_sem.at[t, ch, a, n],
            q_rsem.at[side, a, t, ch, j], to,
        )

    def gather_copy(t, ch, d):
        return copy(
            dz.at[t, ch, i], dz.at[t, ch, i], z_sem.at[t, ch, d], z_rsem.at[t, ch, i],
            {"pre": lax.rem(i + d, pre)},
        )

    def is_me(m, h):
        return jnp.logical_and(m == i, h == j)

    def delta_copy(t, ch, to_i):
        return copy(
            dsend.at[ch], dbuf.at[0, a_me, t, ch, j], d_sem.at[ch, to_i], d_rsem.at[ch, a_me, j],
            {"pre": to_i, "post": j_me},
        )

    def final_copy(ch, to_i):
        return copy(
            fbuf.at[1, 0, 0, ch], fbuf.at[0, a_me, j, ch], f_sem.at[ch, to_i], f_rsem.at[ch, a_me, j],
            {"pre": to_i, "post": j_me},
        )

    def wait_slot(ref, sem):
        copy(ref, ref, sem, sem, other).wait_recv()

    gain = None
    def send_part(t, ch, m, now):
        psend[t, ch, m] = jnp.dot(now, wbuf[m], preferred_element_type=F32).astype(BF16)
        part_copy(t, ch, m).start()

    def own_part(t, ch, now):
        precv[t, ch, i] = jnp.dot(now, wbuf[i], preferred_element_type=F32).astype(BF16)

    reach = [d for d in range(2, pre)] + [1]
    for t in range(STEPS):
        if t == 0:
            for a in range(ppp):
                part = jnp.dot(rates_ref[...], w_ref[a], preferred_element_type=F32)
                for h in range(post):
                    for ch in range(chains):
                        top = h * rows + ch * rh
                        value = part[top:top + rh].astype(BF16)
                        here = is_me(ppp * j + a, h)

                        @pl.when(here)
                        def _():
                            precv[0, ch, i] = value

                        @pl.when(jnp.logical_not(here))
                        def _():
                            psend[0, ch, a * post + h] = value
                            first_copy(ch, a, h).start()

            for a in range(ppp):
                wbuf[j * ppp + a] = w_ref[a]
        elif t == 1:
            nexts = [one_block(rbuf[0, 1, ch, j]) for ch in range(chains)]
            for d in range(post):
                h = lax.rem(j + d, post)
                if d > 0:
                    for a in range(ppp):
                        wait_slot(wbuf.at[h * ppp + a, band], w_rsem.at[h * ppp + a])
                        weight_swap(h, a).start()
                for a in range(ppp):
                    m = h * ppp + a
                    if d > 0:
                        wait_slot(wbuf.at[m, band], wx_rsem.at[m])
                    for ch in range(chains):
                        @pl.when(m != i)
                        def _():
                            send_part(1, ch, m, nexts[ch])

                        @pl.when(m == i)
                        def _():
                            own_part(1, ch, nexts[ch])

        for ch in range(chains):
            if t > 1:
                now = one_block(rbuf[0, t, ch, j])
                for d in reach:
                    send_part(t, ch, lax.rem(i + d, pre), now)
                own_part(t, ch, now)
            for back in range(t + 1 if t == 2 else 0 if t < 2 else 1):
                for n in range(1, post * rep):
                    spread_rates(t - back, ch, n).start()
        if t == 0:
            @pl.when(away)
            def _():
                wait_slot(sbuf.at[0], s_rsem.at[0])
                wait_slot(sbuf.at[1], s_rsem.at[1])
                wait_slot(ctbuf, s_rsem.at[2])

            types = ctbuf[...]
            gain = jnp.zeros(types.shape, F32)
            for k in range(gains_ref.shape[0]):
                gain = jnp.where(types == k, gains_ref[k], gain)
            gain = gain[0:1]
        for ch in range(chains):
            if t == 0:
                for m in range(pre):
                    @pl.when(jnp.logical_or(away, m != i))
                    def _():
                        wait_slot(precv.at[0, ch, m], p_rsem.at[0, ch, m])

            else:
                for d in range(1, pre):
                    m = lax.rem(i + d, pre)
                    wait_slot(precv.at[t, ch, m], p_rsem.at[t, ch, m])
            cur = precv[t, ch, 0].astype(F32)
            for m in range(1, pre):
                cur = cur + precv[t, ch, m].astype(F32)
            act = jnp.tanh(gain * cur + sbuf[0, ch].astype(F32))
            acts[t, ch] = act
            curs[t, ch] = cur
            fresh = ((1.0 - LEAK) * rbuf[0, t, ch, j].astype(F32) + LEAK * act).astype(BF16)
            if t < STEPS - 1:
                rbuf[0, t + 1, ch, j] = fresh
            else:
                fbuf[1, 0, 0, ch] = fresh

    errors = [sbuf[1, ch].astype(F32) for ch in range(chains)]
    tally = jnp.zeros((8, n_pre), F32)
    for t in reversed(range(STEPS)):
        for ch in range(chains):
            error = errors[ch]
            act = acts[t, ch]
            du = error * LEAK * (1.0 - act * act)
            delta = (du * gain).astype(BF16)
            if t > 0:
                dz[t, ch, i] = delta
                for d in reach:
                    gather_copy(t, ch, d).start()
            else:
                dsend[ch] = delta
                for m in range(pre):
                    @pl.when(jnp.logical_or(away, m != i))
                    def _():
                        delta_copy(0, ch, m).start()

                @pl.when(home)
                def _():
                    dbuf[0, a_me, 0, ch, j] = dsend[ch]

            weighed = du * curs[t, ch]
            for top in range(0, rh, 8):
                tally = tally + weighed[top:top + 8]
        if t == 0:
            break
        for ch in range(chains):
            back = None
            for d in range(pre):
                m = lax.rem(i + d, pre)
                if d > 0:
                    wait_slot(dz.at[t, ch, m], z_rsem.at[t, ch, m])
                term = lax.dot_general(
                    one_block(dz[t, ch, m]), wbuf[m], (((1,), (1,)), ((), ())), preferred_element_type=F32
                )
                back = term if back is None else back + term
            errors[ch] = (1.0 - LEAK) * errors[ch] + back
            for a in range(ppp):
                for n in range(1, post * rep):
                    spread_delta(t, ch, a, n).start()
                dbuf[0, a, t, ch, j] = dz[t, ch, j * ppp + a]

    kinds = grecv.shape[-1]
    hot = (lax.broadcasted_iota(jnp.int32, (kinds, n_pre), 0) == ctbuf[0:1]).astype(F32)
    grecv[me] = lax.dot_general(
        tally, hot, (((1,), (1,)), ((), ())), preferred_element_type=F32, precision=lax.Precision.HIGHEST
    )

    def gain_copy(n):
        return copy(grecv.at[me], grecv.at[me], g_sem.at[n], g_rsem.at[me], where_is(peer(n)))

    def send_gain(n, carry):
        gain_copy(n).start()
        return carry

    lax.fori_loop(1, group, send_gain, 0)

    for ch in range(chains):
        for m in range(pre):
            @pl.when(jnp.logical_or(away, m != i))
            def _():
                final_copy(ch, m).start()

        @pl.when(home)
        def _():
            fbuf[0, a_me, j, ch] = fbuf[1, 0, 0, ch]

    for t in range(STEPS):
        for ch in range(chains):
            for n in range(1, post * rep):
                h, side = cross(n)
                wait_slot(rbuf.at[side, t, ch, h], r_rsem.at[side, t, ch, h])
                if t > 0:
                    for a in range(ppp):
                        wait_slot(dbuf.at[side, a, t, ch, h], q_rsem.at[side, a, t, ch, h])

    def outer(side, low, high, a):
        lead = (high - low) * chains * post
        return lax.dot_general(
            flat_rows(rbuf[side, low:high], lead), flat_rows(dbuf[side, a, low:high], lead),
            (((0,), (0,)), ((), ())), preferred_element_type=F32,
        )

    for a in range(ppp):
        cols = slice(a * n_pre, (a + 1) * n_pre)
        g_ref[:, cols] = outer(0, 1, STEPS, a) + outer(1, 1, STEPS, a)
    for ch in range(chains):
        for a in range(ppp):
            for h in range(post):
                @pl.when(jnp.logical_not(is_me(ppp * j + a, h)))
                def _():
                    wait_slot(dbuf.at[0, a, 0, ch, h], d_rsem.at[ch, a, h])

            swap_delta(0, ch, a).start()
    for a in range(ppp):
        cols = slice(a * n_pre, (a + 1) * n_pre)
        for ch in range(chains):
            swap_delta(0, ch, a).wait_recv()
        g_ref[:, cols] += outer(0, 0, 1, a) + outer(1, 0, 1, a)

    for a in range(ppp):
        for h in range(post):
            for ch in range(chains):
                @pl.when(jnp.logical_not(is_me(ppp * j + a, h)))
                def _():
                    wait_slot(fbuf.at[0, a, h, ch], f_rsem.at[ch, a, h])

        final_ref[:, a * n_pre:(a + 1) * n_pre] = flat_rows(fbuf[0, a], post * chains)

    def take_gain(n, carry):
        source = peer(n)
        wait_slot(grecv.at[source], g_rsem.at[source])
        return carry

    lax.fori_loop(1, group, take_gain, 0)
    gathered = grecv[0]
    for n in range(1, group):
        gathered = gathered + grecv[n]
    gg_ref[...] = jnp.sum(gathered, axis=0, keepdims=True)[:, :gg_ref.shape[1]]

    for h in range(post):
        @pl.when(jnp.logical_and(home, h != j))
        def _():
            for one in share_copies(h):
                one.wait_send()

    for d in range(1, post):
        h = lax.rem(j + d, post)
        for a in range(ppp):
            weight_copy(d, a).wait_send()
            weight_swap(h, a).wait_send()
    for t in range(STEPS):
        for ch in range(chains):
            for d in reach:
                if t > 0:
                    part_copy(t, ch, lax.rem(i + d, pre)).wait_send()
                    gather_copy(t, ch, d).wait_send()
            for n in range(1, post * rep):
                spread_rates(t, ch, n).wait_send()
                if t > 0:
                    for a in range(ppp):
                        spread_delta(t, ch, a, n).wait_send()
    for ch in range(chains):
        for a in range(ppp):
            swap_delta(0, ch, a).wait_send()
            for h in range(post):
                @pl.when(jnp.logical_not(is_me(ppp * j + a, h)))
                def _():
                    first_copy(ch, a, h).wait_send()

        for m in range(pre):
            @pl.when(jnp.logical_or(away, m != i))
            def _():
                delta_copy(0, ch, m).wait_send()
                final_copy(ch, m).wait_send()

    def end_gain(n, carry):
        gain_copy(n).wait_send()
        return carry

    lax.fori_loop(1, group, end_gain, 0)


def body(rates0, stimulus, cotangent, weights, src_block, dst_block, live_count, cell_type, gains):
    pre, post, rep = lax.axis_size("pre"), lax.axis_size("post"), lax.axis_size("rep")
    batch, n_pre = rates0.shape
    n_post = stimulus.shape[1]
    slots, width = weights.shape[2], weights.shape[3]
    ppp = pre // post
    chains = 1
    rh = batch // (chains * post)
    group = pre * post * rep
    smem = pl.BlockSpec(memory_space=pltpu.SMEM)
    vmem = pl.BlockSpec(memory_space=pltpu.VMEM)

    dense = pl.pallas_call(
        build_kernel,
        grid=(slots // CHUNK,),
        out_shape=jax.ShapeDtypeStruct((ppp, n_pre, n_pre), BF16),
        in_specs=[smem, smem, smem, pl.BlockSpec((1, 1, CHUNK, width, width), lambda p: (0, 0, p, 0, 0))],
        out_specs=pl.BlockSpec((ppp, n_pre, n_pre), lambda p: (0, 0, 0)),
        scratch_shapes=[pltpu.VMEM((ppp, n_pre, n_pre), F32)],
        compiler_params=pltpu.CompilerParams(vmem_limit_bytes=32 * 2**20),
        name="dense_tile",
    )(src_block, dst_block, live_count, weights)

    dma = pltpu.SemaphoreType.DMA
    V = pltpu.VMEM
    final, gain_grad, dense_grad = pl.pallas_call(
        functools.partial(step_kernel, (pre, post, rep, chains, rh, n_pre)),
        out_shape=(
            jax.ShapeDtypeStruct((batch, n_post), BF16),
            jax.ShapeDtypeStruct((1, gains.shape[0]), F32),
            jax.ShapeDtypeStruct((n_pre, n_post), F32),
        ),
        in_specs=[vmem, vmem, vmem, vmem, vmem, smem],
        out_specs=(vmem, vmem, vmem),
        scratch_shapes=[
            V((pre, n_pre, n_pre), BF16),
            V((2, STEPS, chains, post, rh, n_pre), BF16),
            V((2, ppp, STEPS, chains, post, rh, n_pre), BF16),
            V((STEPS, chains, pre, rh, n_pre), BF16),
            V((2, ppp, post, chains, rh, n_pre), BF16),
            V((STEPS, chains, pre, rh, n_pre), BF16),
            V((STEPS, chains, pre, rh, n_pre), BF16),
            V((chains, rh, n_pre), BF16),
            V((2, post, chains, rh, n_pre), BF16),
            V((2, chains, rh, n_pre), BF16),
            V((8, n_pre), jnp.int32),
            V((8, n_pre), jnp.int32),
            V((group, 8, 128), F32),
            V((STEPS, chains, rh, n_pre), F32),
            V((STEPS, chains, rh, n_pre), F32),
            dma((post, ppp)), dma((pre,)), dma((pre,)), dma((pre,)),
            dma((post, 3)), dma((3,)),
            dma((STEPS, chains, pre)), dma((STEPS, chains, pre)),
            dma((STEPS, chains, post * rep)), dma((rep, STEPS, chains, post)),
            dma((STEPS, chains, pre)), dma((STEPS, chains, pre)),
            dma((STEPS, chains, ppp, post * rep)), dma((rep, ppp, STEPS, chains, post)),
            dma((chains, pre)), dma((chains, ppp, post)),
            dma((chains, pre)), dma((chains, ppp, post)),
            dma((chains, ppp)), dma((chains, ppp)),
            dma((group,)), dma((group,)),
        ],
        compiler_params=pltpu.CompilerParams(
            collective_id=0, has_side_effects=True, vmem_limit_bytes=48 * 2**20
        ),
        name="window",
    )(rates0, stimulus, cotangent, dense, cell_type.reshape(1, n_post), gains)

    share = slots // rep
    grad = pl.pallas_call(
        emit_kernel,
        out_shape=jax.ShapeDtypeStruct((1, 1, share, width, width), F32),
        in_specs=[smem, smem, smem, vmem],
        out_specs=pl.BlockSpec(memory_space=pl.ANY),
        scratch_shapes=[V((width, width), F32), dma((share,))],
        compiler_params=pltpu.CompilerParams(vmem_limit_bytes=32 * 2**20),
        name="emit_slots",
    )(src_block, dst_block, live_count, dense_grad)
    return final, grad, gain_grad.reshape(gains.shape)


def solution(mesh):
    return jax.shard_map(
        body,
        mesh=mesh,
        in_specs=(
            P(("groups", "rep"), "pre"),
            P(("groups", "rep"), "post"),
            P(("groups", "rep"), "post"),
            P(("groups", "pre"), "post", None, None, None),
            P(("groups", "pre"), "post", None),
            P(("groups", "pre"), "post", None),
            P(("groups", "pre"), "post"),
            P(("groups", "post")),
            P(),
        ),
        out_specs=(
            P(("groups", "rep"), "post"),
            P(("groups", "pre"), "post", "rep", None, None),
            P("groups"),
        ),
        check_vma=False,
    )
```
